256 devices in a mesh: dp: 8 (over z), fsdp: 32 (over y, x, core).
Axes of the slice: x: 4, y: 4, z: 8, core: 2. Of those that a mesh axis runs over, the one named last changes fastest.
Arguments:
- tokens: bfloat16 [65536, 8192], P(('dp', 'fsdp')), may hold values from -17 to 17
- output_gradient: bfloat16 [65536, 1024], P(('dp', 'fsdp')), may hold values from -17 to 17
- base_weight: bfloat16 [8192, 1024], P('fsdp'), may hold values from -0.0625 to 0.0625
- down_matrices: bfloat16 [8192, 128], replicated, may hold values from -0.0625 to 0.0625
- up_matrices: bfloat16 [1024, 128], replicated, may hold values from -0.1875 to 0.1875
- master_a: float32 [8192, 128], P(('dp', 'fsdp')), may hold values from -0.0625 to 0.0625
- moment_a: float32 [8192, 128], P(('dp', 'fsdp')), may hold values from -0.6 to 0.6
- second_a: float32 [8192, 128], P(('dp', 'fsdp')), may hold values from 0.5 to 2
- master_b: float32 [1024, 128], P(('dp', 'fsdp')), may hold values from -0.1875 to 0.1875
- moment_b: float32 [1024, 128], P(('dp', 'fsdp')), may hold values from -0.6 to 0.6
- second_b: float32 [1024, 128], P(('dp', 'fsdp')), may hold values from 0.5 to 2
- seg_counts: int32 [256, 8], P(('dp', 'fsdp')), may hold values from 1 to 128, 256 in all within a row
- bad_flags: int32 [256, 8], P(('dp', 'fsdp')), may hold values from 0 to 1, as said below
Outputs:
- input_gradient: bfloat16 [65536, 8192], P(('dp', 'fsdp'))
- new_master_a: float32 [8192, 128], P(('dp', 'fsdp'))
- new_moment_a: float32 [8192, 128], P(('dp', 'fsdp'))
- new_second_a: float32 [8192, 128], P(('dp', 'fsdp'))
- new_master_b: float32 [1024, 128], P(('dp', 'fsdp'))
- new_moment_b: float32 [1024, 128], P(('dp', 'fsdp'))
- new_second_b: float32 [1024, 128], P(('dp', 'fsdp'))
The draws below stay inside these ranges and needn't reach their ends.
Inputs may be any that keep to these rules, and one draw needn't show every extreme that they name: `seg_counts`: each device's row sums to 256, and its largest entry is exactly 128. `bad_flags`: exactly 8 // 2 adapters are flagged, each by exactly one device.
All inputs are finite; a program needn't handle non-finite values.
Results may differ from the reference program's by a relative error of at most 0.002.
Values may be sent and summed in bfloat16 or wider, within the bound.
No kernel may reach another device: no remote copies, remote signals or barrier semaphores. Data moves between devices by JAX's collectives and lax.ppermute only.
A program may use at most 128 MiB of HBM per device.

```python
import math
import jax
import jax.numpy as jnp
import numpy as np
from jax import lax

D = 8192
KV = 1024
RANK = 16
ADAPTERS = 8
TOK_DEV = 256
TOKENS = 65536
MOST = 128
COLS = 128
DEVICES = 256


def column_levels(noise, key_level, key_rough, block_width, level_lo, level_hi):
    col_count = noise.shape[1]
    block_count = col_count // block_width
    level = jnp.exp(jax.random.uniform(key_level, (block_count,), jnp.float32, math.log(level_lo), math.log(level_hi)))
    col_level = jnp.repeat(level, block_width, total_repeat_length=col_count)
    rough = jnp.exp(jax.random.uniform(key_rough, (col_count,), jnp.float32, -0.3, 0.3))
    values = noise * (col_level * rough)[None, :]
    return values.astype(jnp.bfloat16)


def draw_tokens(key, part):
    key = jax.random.fold_in(key, 3)
    key_noise, key_level, key_rough = jax.random.split(key, 3)
    noise = jax.random.truncated_normal(key_noise, -4.0, 4.0, (TOKENS, D), jnp.float32)
    return column_levels(noise, key_level, key_rough, D // DEVICES, 0.3, 3.0)


def draw_output_gradient(key, part):
    key = jax.random.fold_in(key, 5)
    key_noise, key_level, key_rough = jax.random.split(key, 3)
    noise = jax.random.truncated_normal(key_noise, -4.0, 4.0, (TOKENS, KV), jnp.float32)
    return column_levels(noise, key_level, key_rough, KV // DEVICES, 0.3, 3.0)


def draw_bad_flags(key, part):
    key = jax.random.fold_in(key, 11)
    key_owner, key_order = jax.random.split(key)
    flag_owner = jax.random.randint(key_owner, (ADAPTERS,), 0, DEVICES)
    order = jax.random.permutation(key_order, ADAPTERS)
    flagged = order < ADAPTERS // 2
    device_ids = jnp.arange(DEVICES, dtype=jnp.int32)[:, None]
    return ((device_ids == flag_owner[None, :]) & flagged[None, :]).astype(jnp.int32)


def shard_levels(rng, dims, cuts, least, largest):
    def one(axis_at, parts):
        heights = jax.random.uniform(jax.random.fold_in(jax.random.fold_in(rng, 6), axis_at), (parts,), jnp.float32, least / len(cuts), largest / len(cuts))
        return jnp.repeat(jnp.exp(heights), dims[axis_at] // parts).reshape((-1,) + (1,) * (len(dims) - axis_at - 1))

    loudness = one(*cuts[0])
    for cut in cuts[1:]:
        loudness = loudness * one(*cut)
    return loudness


def split_up(number_of, total, reach, slope):
    portions = [(1 << 20) // math.isqrt(rank ** slope) + 1 for rank in range(2, number_of + 1)]
    surplus, holding = total - reach - (number_of - 1), [1] * (number_of - 1)
    while surplus > 0:
        movable = [i for i in range(number_of - 1) if holding[i] < reach]
        whole, budget = sum([portions[i] for i in movable]), surplus
        for i in movable:
            extra = min(reach - holding[i], max(1, budget * portions[i] // whole), surplus)
            holding[i] = holding[i] + extra
            surplus = surplus - extra
    return np.array([reach] + holding)


def ragged_sizes(key, amount, total, most, skew):
    if amount == 2:
        one = jax.random.randint(key, (), max(1, total - most), min(most, total - 1) + 1)
        return jnp.stack([one, total - one])
    lengths = jnp.asarray(split_up(amount, total, most, skew), jnp.int32)
    couples = (amount - 1) // 2
    source_of, receiver = lengths[1:1 + 2 * couples:2], lengths[2:2 + 2 * couples:2]
    margin = jnp.minimum(source_of - 1, most - receiver)
    moved = jax.random.randint(jax.random.fold_in(key, 1), (couples,), 0, 1 << 20) % (margin + 1)
    lengths = lengths.at[1:1 + 2 * couples:2].set(source_of - moved).at[2:2 + 2 * couples:2].set(receiver + moved)
    return lengths[jax.random.permutation(jax.random.fold_in(key, 2), amount)]


def centred(key, extent, scale, most, cuts=(), kind=jnp.bfloat16):
    result = jax.random.normal(key, extent, jnp.float32) * scale
    if len(cuts) > 0:
        result = shard_levels(key, extent, cuts, -0.22, 0.18) * result
    return jnp.clip(result, min=-most, max=most).astype(kind)


def setup_inputs(seed: int = 0) -> dict:
    arg_keys = jax.random.split(jax.random.key(seed), 14)
    return {
        "tokens": draw_tokens(jax.random.fold_in(arg_keys[13], 71), 0),
        "output_gradient": draw_output_gradient(jax.random.fold_in(arg_keys[13], 71), 0),
        "base_weight": centred(arg_keys[2], (D, KV), D ** -0.5, 0.0625, ((0, 32),)),
        "down_matrices": centred(arg_keys[3], (D, COLS), D ** -0.5, 0.0625),
        "up_matrices": centred(arg_keys[4], (KV, COLS), KV ** -0.5, 0.1875),
        "master_a": centred(arg_keys[5], (D, COLS), D ** -0.5, 0.0625, ((0, 256),), jnp.float32),
        "moment_a": centred(arg_keys[6], (D, COLS), 0.1, 0.6, ((0, 256),), jnp.float32),
        "second_a": jnp.clip(jnp.exp(math.log(2.0) - 1.3862944 * jax.random.uniform(arg_keys[7], (D, COLS), jnp.float32) ** shard_levels(arg_keys[7], (D, COLS), ((0, 256),), -0.2, 0.2)), 0.5, 2.0),
        "master_b": centred(arg_keys[8], (KV, COLS), KV ** -0.5, 0.1875, ((0, 256),), jnp.float32),
        "moment_b": centred(arg_keys[9], (KV, COLS), 0.1, 0.6, ((0, 256),), jnp.float32),
        "second_b": jnp.clip(jnp.exp(math.log(2.0) - 1.3862944 * jax.random.uniform(arg_keys[10], (KV, COLS), jnp.float32) ** shard_levels(arg_keys[10], (KV, COLS), ((0, 256),), -0.2, 0.2)), 0.5, 2.0),
        "seg_counts": jax.vmap(lambda own: ragged_sizes(own, ADAPTERS, TOK_DEV, MOST, 2))(jax.random.split(arg_keys[11], DEVICES)).reshape((DEVICES, ADAPTERS)).astype(jnp.int32),
        "bad_flags": draw_bad_flags(jax.random.fold_in(arg_keys[13], 71), 0),
    }


ADAPTER_SCALE = 2.0
BETA_ONE = 0.9
BETA_TWO = 0.95
LEARN_RATE = 0.002
ADAM_EPS = 1e-08

def owner_columns(counts, row_count, adapter_rank, col_count):
    seg_ends = jnp.cumsum(counts)
    row_ids = jnp.arange(row_count, dtype=jnp.int32)
    row_owner = lax.optimization_barrier(jnp.sum((row_ids[:, None] >= seg_ends[None, :]).astype(jnp.int32), axis=1))
    col_owner = jnp.arange(col_count, dtype=jnp.int32) // adapter_rank
    return (row_owner[:, None] == col_owner[None, :]).astype(jnp.float32)

def adam_commit(master, moment, second, grads, col_clip, col_held):
    clipped = grads * col_clip[None, :]
    new_moment = BETA_ONE * moment + (1.0 - BETA_ONE) * clipped
    new_second = BETA_TWO * second + (1.0 - BETA_TWO) * clipped * clipped
    new_master = master - LEARN_RATE * new_moment / (jnp.sqrt(new_second) + ADAM_EPS)
    keep = col_held[None, :] > 0
    return (jnp.where(keep, master, new_master), jnp.where(keep, moment, new_moment), jnp.where(keep, second, new_second))

def reference(tokens, output_gradient, base_weight, down_matrices, up_matrices, master_a, moment_a, second_a, master_b, moment_b, second_b, seg_counts, bad_flags):
    x_blocks = tokens.reshape(DEVICES, TOK_DEV, D)
    g_blocks = output_gradient.reshape(DEVICES, TOK_DEV, KV)

    def one_block(carry, inputs):
        acc_a, acc_b = carry
        input_row_slice, gradient_row_slice, counts = inputs
        ownership_mask = owner_columns(counts, TOK_DEV, RANK, COLS)
        lowrank_product = (ADAPTER_SCALE * jnp.dot(input_row_slice, down_matrices, preferred_element_type=jnp.float32) * ownership_mask).astype(jnp.bfloat16)
        backward_product = (ADAPTER_SCALE * jnp.dot(gradient_row_slice, up_matrices, preferred_element_type=jnp.float32) * ownership_mask).astype(jnp.bfloat16)
        frozen_portion = jnp.dot(gradient_row_slice, base_weight.T, preferred_element_type=jnp.float32)
        adapter_portion = jnp.dot(backward_product, down_matrices.T, preferred_element_type=jnp.float32)
        row_gradients = (frozen_portion + adapter_portion).astype(jnp.bfloat16)
        acc_a = acc_a + jnp.dot(input_row_slice.T, backward_product, preferred_element_type=jnp.float32)
        acc_b = acc_b + jnp.dot(gradient_row_slice.T, lowrank_product, preferred_element_type=jnp.float32)
        return ((acc_a, acc_b), row_gradients)
    start = (jnp.zeros((D, COLS), jnp.float32), jnp.zeros((KV, COLS), jnp.float32))
    (grad_a, grad_b), row_gradients = lax.scan(one_block, start, (x_blocks, g_blocks, seg_counts))
    input_gradient = row_gradients.reshape(TOKENS, D)
    col_squares = lax.optimization_barrier(jnp.sum(grad_a * grad_a, axis=0)) + lax.optimization_barrier(jnp.sum(grad_b * grad_b, axis=0))
    sum_squares = lax.optimization_barrier(jnp.sum(col_squares.reshape(ADAPTERS, RANK), axis=1))
    limit = jnp.sqrt(jnp.float32(RANK * (D + KV)))
    clip = limit / jnp.maximum(jnp.sqrt(sum_squares), limit)
    held_back = lax.optimization_barrier(jnp.max(bad_flags, axis=0))
    col_clip = jnp.repeat(clip, RANK)
    col_held = jnp.repeat(held_back, RANK)
    new_a = adam_commit(master_a, moment_a, second_a, grad_a, col_clip, col_held)
    new_b = adam_commit(master_b, moment_b, second_b, grad_b, col_clip, col_held)
    return (input_gradient, new_a[0], new_a[1], new_a[2], new_b[0], new_b[1], new_b[2])
```

```python
import functools

import jax
import jax.numpy as jnp
from jax import lax
from jax.experimental import pallas as pl
from jax.experimental.pallas import tpu as pltpu
from jax.sharding import Mesh
from jax.sharding import PartitionSpec as P

ADAPTER_SCALE = 2.0
BETA_ONE = 0.9
BETA_TWO = 0.95
LEARN_RATE = 0.002
ADAM_EPS = 1e-08

DEV = ("z", "y", "x", "c")
PLANE = ("y", "x", "c")
F32 = jnp.float32
BF16 = jnp.bfloat16
CONTRACT_LAST = (((1,), (1,)), ((), ()))
CONTRACT_FIRST = (((0,), (0,)), ((), ()))

VMEM = pl.BlockSpec(memory_space=pltpu.VMEM)
SMEM = pl.BlockSpec(memory_space=pltpu.SMEM)
HBM = pl.BlockSpec(memory_space=pl.ANY)


def call(kernel, outs, ins, scratch=(), limit=48, flops=0, nbytes=0):
    return pl.pallas_call(
        kernel,
        out_shape=outs,
        in_specs=ins,
        out_specs=jax.tree.map(lambda _: VMEM, outs),
        scratch_shapes=list(scratch),
        compiler_params=pltpu.CompilerParams(vmem_limit_bytes=limit << 20),
        cost_estimate=pl.CostEstimate(flops=flops, bytes_accessed=nbytes, transcendentals=0),
    )


def grads_kernel(
    where_ref, counts_ref, tok_hbm, g_hbm, down_hbm, up_hbm,
    keep_ref, send_ref, back_ref,
    tok, g, down, up, sems, small_sems,
):
    rows, width = tok.shape
    kv = g.shape[1]
    cols = down.shape[1]
    adapters = counts_ref.shape[1]
    rank = cols // adapters
    tiles = sems.shape[0]
    tile = width // tiles
    blocks = keep_ref.shape[0]
    block = width // blocks
    kv_block = kv // blocks
    half = block // 8
    mine = where_ref[3]

    g_copy = pltpu.make_async_copy(g_hbm, g, small_sems.at[0])
    up_copy = pltpu.make_async_copy(up_hbm, up, small_sems.at[1])
    g_copy.start()
    up_copy.start()
    tok_copies = []
    for t in range(tiles):
        span = pl.ds(t * tile, tile)
        a = pltpu.make_async_copy(tok_hbm.at[:, span], tok.at[:, span], sems.at[t, 0])
        b = pltpu.make_async_copy(down_hbm.at[span, :], down.at[span, :], sems.at[t, 1])
        a.start()
        b.start()
        tok_copies.append((a, b))

    row_ids = lax.broadcasted_iota(jnp.int32, (rows, cols), 0)
    col_owner = lax.broadcasted_iota(jnp.int32, (rows, cols), 1) // rank
    owner = jnp.zeros((rows, cols), jnp.int32)
    end = jnp.int32(0)
    for e in range(adapters):
        end = end + counts_ref[0, e]
        owner = owner + (row_ids >= end).astype(jnp.int32)
    mask = (owner == col_owner).astype(F32)

    g_copy.wait()
    up_copy.wait()
    back = (
        ADAPTER_SCALE * jnp.dot(g[...], up[...], preferred_element_type=F32) * mask
    ).astype(BF16)
    back_ref[...] = back

    acc = jnp.zeros((rows, cols), F32)
    for t in range(tiles):
        tok_copies[t][0].wait()
        tok_copies[t][1].wait()
        span = slice(t * tile, (t + 1) * tile)
        acc = acc + jnp.dot(tok[:, span], down[span, :], preferred_element_type=F32)
        for s in range(tile // block):
            b = t * (tile // block) + s
            r = lax.dot_general(
                tok[:, b * block : (b + 1) * block], back, CONTRACT_FIRST,
                preferred_element_type=F32,
            ).reshape(4, 2, half, cols)
            first = mine == 0
            keep_ref[b, : 4 * half] = jnp.where(first, r[:, 0], r[:, 1]).reshape(4 * half, cols)
            send_ref[b, : 4 * half] = jnp.where(first, r[:, 1], r[:, 0]).reshape(4 * half, cols)
    low = (ADAPTER_SCALE * acc * mask).astype(BF16)
    group = 256 // kv_block
    for s in range(kv // 256):
        r = lax.dot_general(
            g[:, s * 256 : (s + 1) * 256], low, CONTRACT_FIRST, preferred_element_type=F32
        ).reshape(group, kv_block, cols)
        keep_ref[s * group : (s + 1) * group, 4 * half :] = r
        send_ref[s * group : (s + 1) * group, 4 * half :] = r


def to_z_kernel(where_ref, keep_ref, recv_ref, *outs):
    count = len(outs)
    me = where_ref[0]
    per = keep_ref.shape[0] // count
    for k in range(count):
        to = lax.rem(me + k, count) * per
        for j in range(per):
            rows = keep_ref.shape[1]
            total = keep_ref[to + j] + recv_ref[to + j]
            outs[k][j * rows : (j + 1) * rows] = total.astype(outs[k].dtype)


def to_y_kernel(where_ref, *refs):
    ins, outs = refs[:-4], refs[-4:]
    me = where_ref[1]
    rows = outs[0].shape[0]
    for k in range(4):
        span = pl.ds(pl.multiple_of(lax.rem(me + k, 4) * rows, rows), rows)
        total = ins[0][span]
        for r in ins[1:]:
            total = total + r[span].astype(F32)
        outs[k][...] = total


def to_x_kernel(flags_ref, a, b, c, d, out):
    rows = a.shape[0]
    cols = a.shape[1]
    adapters = flags_ref.shape[1]
    rank = cols // adapters
    out[:rows] = (a[...] + b[...]) + (c[...] + d[...])
    owner = lax.broadcasted_iota(jnp.int32, (8, cols), 1) // rank
    flags = jnp.zeros((8, cols), F32)
    for e in range(adapters):
        flags = jnp.where(owner == e, flags_ref[0, e].astype(F32), flags)
    out[rows:] = flags


def squares_kernel(where_ref, a, b, c, d, total_ref, squares_ref):
    rows = total_ref.shape[0]
    cols = total_ref.shape[1]
    wide = rows * 4 // 5
    total = (a[...] + b[...]) + (c[...] + d[...])
    total_ref[...] = total[:rows]
    part_a = total[:wide]
    part_b = total[wide:rows]
    owner = (lax.broadcasted_iota(jnp.int32, part_b.shape, 0) // 4) % 2
    part_b = jnp.where(owner == where_ref[3], part_b, 0.0)
    squares = jnp.sum(part_a * part_a, axis=0, keepdims=True) + jnp.sum(
        part_b * part_b, axis=0, keepdims=True
    )
    row = lax.broadcasted_iota(jnp.int32, (8, cols), 0)
    squares_ref[...] = jnp.where(row == 0, squares, total[rows:])


def adam_kernel(
    limit_sq, where_ref, total_ref, squares_ref,
    master_a, moment_a, second_a, master_b, moment_b, second_b,
    out_ma, out_oa, out_sa, out_mb, out_ob, out_sb,
):
    rows, cols = master_a.shape
    adapters = 8
    rank = cols // adapters
    col_squares = squares_ref[0:1]
    flags = squares_ref[1:2]
    owner = lax.broadcasted_iota(jnp.int32, (1, cols), 1) // rank
    sums = jnp.zeros((1, cols), F32)
    for e in range(adapters):
        one = jnp.sum(jnp.where(owner == e, col_squares, 0.0), axis=1, keepdims=True)
        sums = jnp.where(owner == e, one, sums)
    limit = jnp.sqrt(jnp.full((1, cols), limit_sq, F32))
    clip = limit / jnp.maximum(jnp.sqrt(sums), limit)
    held = flags > 0.5

    def commit(grad, master, moment, second, to_master, to_moment, to_second):
        clipped = grad * clip
        m, o, s = master[...], moment[...], second[...]
        new_o = BETA_ONE * o + (1.0 - BETA_ONE) * clipped
        new_s = BETA_TWO * s + (1.0 - BETA_TWO) * clipped * clipped
        new_m = m - LEARN_RATE * new_o / (jnp.sqrt(new_s) + ADAM_EPS)
        to_master[...] = jnp.where(held, m, new_m)
        to_moment[...] = jnp.where(held, o, new_o)
        to_second[...] = jnp.where(held, s, new_s)

    x = where_ref[2]
    grad_a = total_ref[pl.ds(pl.multiple_of(x * rows, rows), rows)]
    pair = total_ref[pl.ds(pl.multiple_of(4 * rows + x * 8, 8), 8)]
    grad_b = jnp.where(where_ref[3] == 0, pair[:4], pair[4:])
    commit(grad_a, master_a, moment_a, second_a, out_ma, out_oa, out_sa)
    commit(grad_b, master_b, moment_b, second_b, out_mb, out_ob, out_sb)


def input_grad_kernel(g, weight, back, down, out):
    total = lax.dot_general(g[...], weight[...], CONTRACT_LAST, preferred_element_type=F32)
    total = total + lax.dot_general(
        back[...], down[...], CONTRACT_LAST, preferred_element_type=F32
    )
    out[...] = total.astype(out.dtype)


def input_grad(g, weight, back, down, tile):
    rows, kv = g.shape
    width, cols = down.shape
    return pl.pallas_call(
        input_grad_kernel,
        grid=(width // tile,),
        out_shape=jax.ShapeDtypeStruct((rows, width), BF16),
        in_specs=[
            pl.BlockSpec((rows, kv), lambda i: (0, 0)),
            pl.BlockSpec((tile, kv), lambda i: (i, 0)),
            pl.BlockSpec((rows, cols), lambda i: (0, 0)),
            pl.BlockSpec((tile, cols), lambda i: (i, 0)),
        ],
        out_specs=pl.BlockSpec((rows, tile), lambda i: (0, i)),
        compiler_params=pltpu.CompilerParams(vmem_limit_bytes=32 << 20),
        cost_estimate=pl.CostEstimate(
            flops=2 * rows * width * (kv + cols),
            bytes_accessed=2 * width * (kv + cols + rows),
            transcendentals=0,
        ),
    )(g, weight, back, down)


def shift(value, axis, size, by):
    return lax.ppermute(value, axis, [(i, (i + by) % size) for i in range(size)])


def flip(value, axis, size, bit):
    return lax.ppermute(value, axis, [(i, i ^ bit) for i in range(size)])


def shards(sizes, tokens, g, base_weight, down, up, ma, oa, sa, mb, ob, sb, counts, flags):
    nz, ny, nx, nc = sizes
    rows, width = tokens.shape
    kv = g.shape[1]
    cols = down.shape[1]
    where = jnp.stack([lax.axis_index(a) for a in DEV]).astype(jnp.int32)
    sds = jax.ShapeDtypeStruct

    weight = lax.all_gather(base_weight, PLANE, axis=0, tiled=True)

    blocks = nz * ny
    deep = width // blocks // nc + kv // blocks
    part = sds((blocks, deep, cols), F32)
    tiles = 8
    keep, send, back = call(
        grads_kernel,
        (part, part, sds((rows, cols), BF16)),
        [SMEM, SMEM, HBM, HBM, HBM, HBM],
        [
            pltpu.VMEM((rows, width), BF16),
            pltpu.VMEM((rows, kv), BF16),
            pltpu.VMEM((width, cols), BF16),
            pltpu.VMEM((kv, cols), BF16),
            pltpu.SemaphoreType.DMA((tiles, 2)),
            pltpu.SemaphoreType.DMA((2,)),
        ],
        flops=4 * rows * width * cols,
        nbytes=12 << 20,
    )(where, counts, tokens, g, down, up)

    recv = flip(send, "c", nc, 1)
    z_rows = ny * deep
    out_z = tuple(sds((z_rows, cols), F32 if k == 0 else BF16) for k in range(nz))
    to_z = call(to_z_kernel, out_z, [SMEM, VMEM, VMEM], nbytes=6 << 20)(where, keep, recv)
    from_z = [to_z[0]] + [shift(to_z[k], "z", nz, k) for k in range(1, nz)]
    out_y = tuple(sds((deep, cols), F32) for _ in range(ny))
    to_y = call(to_y_kernel, out_y, [SMEM] + [VMEM] * nz, nbytes=2 << 20)(where, *from_z)
    from_y = [to_y[0]] + [shift(to_y[k], "y", ny, k) for k in range(1, ny)]
    to_x = call(to_x_kernel, sds((deep + 8, cols), F32), [SMEM] + [VMEM] * ny)(flags, *from_y)
    from_x = [to_x] + [shift(to_x, "x", nx, k) for k in range(1, nx)]
    total, squares = call(
        squares_kernel, (sds((deep, cols), F32), sds((8, cols), F32)), [SMEM] + [VMEM] * nx
    )(where, *from_x)
    for axis, size in (("c", nc), ("y", ny), ("z", nz)):
        bit = 1
        while bit < size:
            squares = squares + flip(squares, axis, size, bit)
            bit *= 2

    shape = lambda v: sds(v.shape, v.dtype)
    new = call(
        functools.partial(adam_kernel, float(cols // 8 * (width + kv))),
        tuple(shape(v) for v in (ma, oa, sa, mb, ob, sb)),
        [SMEM] + [VMEM] * 8,
    )(where, total, squares, ma, oa, sa, mb, ob, sb)
    out = input_grad(g, weight, back, down, 512)
    return (out, *new)


def solution(mesh):
    sizes = (8, 4, 4, 2)
    fine = Mesh(mesh.devices.reshape(sizes), DEV)
    split = P(DEV, None)
    return jax.shard_map(
        functools.partial(shards, sizes),
        mesh=fine,
        in_specs=(split, split, P(PLANE, None), P(), P()) + (split,) * 8,
        out_specs=(split,) * 7,
        check_vma=False,
    )
```

```python
import functools

import jax
import jax.numpy as jnp
from jax import lax
from jax.experimental import pallas as pl
from jax.experimental.pallas import tpu as pltpu
from jax.sharding import Mesh
from jax.sharding import PartitionSpec as P

ADAPTER_SCALE = 2.0
BETA_ONE = 0.9
BETA_TWO = 0.95
LEARN_RATE = 0.002
ADAM_EPS = 1e-08

DEV = ("z", "y", "x", "c")
PLANE = ("y", "x", "c")
F32 = jnp.float32
BF16 = jnp.bfloat16
CONTRACT_LAST = (((1,), (1,)), ((), ()))
CONTRACT_FIRST = (((0,), (0,)), ((), ()))

VMEM = pl.BlockSpec(memory_space=pltpu.VMEM)
SMEM = pl.BlockSpec(memory_space=pltpu.SMEM)
HBM = pl.BlockSpec(memory_space=pl.ANY)


def call(kernel, outs, ins, scratch=(), limit=48, flops=0, nbytes=0, to=None):
    return pl.pallas_call(
        kernel,
        out_shape=outs,
        in_specs=ins,
        out_specs=jax.tree.map(lambda _: VMEM, outs) if to is None else to,
        scratch_shapes=list(scratch),
        compiler_params=pltpu.CompilerParams(vmem_limit_bytes=limit << 20),
        cost_estimate=pl.CostEstimate(flops=flops, bytes_accessed=nbytes, transcendentals=0),
    )


def grads_kernel(
    where_ref, counts_ref, tok_hbm, g_hbm, down_hbm, up_hbm,
    keep_hbm, send_hbm, back_ref,
    tok, g, down, up, keep_ref, send_ref, sems, small_sems, out_sems,
):
    rows, width = tok.shape
    kv = g.shape[1]
    cols = down.shape[1]
    adapters = counts_ref.shape[1]
    rank = cols // adapters
    tiles = sems.shape[0]
    tile = width // tiles
    blocks, nx = keep_ref.shape[:2]
    block = width // blocks
    half = block // nx // 2
    few = kv // blocks // nx
    first = where_ref[3] == 0

    g_copy = pltpu.make_async_copy(g_hbm, g, small_sems.at[0])
    up_copy = pltpu.make_async_copy(up_hbm, up, small_sems.at[1])
    g_copy.start()
    up_copy.start()
    tok_copies = []
    for t in range(tiles):
        span = pl.ds(t * tile, tile)
        a = pltpu.make_async_copy(tok_hbm.at[:, span], tok.at[:, span], sems.at[t, 0])
        b = pltpu.make_async_copy(down_hbm.at[span, :], down.at[span, :], sems.at[t, 1])
        a.start()
        b.start()
        tok_copies.append((a, b))

    row_ids = lax.broadcasted_iota(jnp.int32, (rows, cols), 0)
    col_owner = lax.broadcasted_iota(jnp.int32, (rows, cols), 1) // rank
    owner = jnp.zeros((rows, cols), jnp.int32)
    end = jnp.int32(0)
    for e in range(adapters):
        end = end + counts_ref[0, e]
        owner = owner + (row_ids >= end).astype(jnp.int32)
    mask = (owner == col_owner).astype(F32)

    g_copy.wait()
    up_copy.wait()
    back = (
        ADAPTER_SCALE * jnp.dot(g[...], up[...], preferred_element_type=F32) * mask
    ).astype(BF16)
    back_ref[...] = back

    acc = jnp.zeros((rows, cols), F32)
    for t in range(tiles):
        tok_copies[t][0].wait()
        tok_copies[t][1].wait()
        span = slice(t * tile, (t + 1) * tile)
        acc = acc + jnp.dot(tok[:, span], down[span, :], preferred_element_type=F32)
    low = (ADAPTER_SCALE * acc * mask).astype(BF16)
    group = block // (few * nx)
    for s in range(kv // block):
        r = lax.dot_general(
            g[:, s * block : (s + 1) * block], low, CONTRACT_FIRST, preferred_element_type=F32
        ).reshape(group, nx, few, cols)
        keep_ref[s * group : (s + 1) * group, :, half:] = r
        send_ref[s * group : (s + 1) * group, :, half:] = r.astype(BF16)
    per = blocks // tiles
    stores = []
    for t in range(tiles):
        for b in range(t * per, (t + 1) * per):
            r = lax.dot_general(
                tok[:, b * block : (b + 1) * block], back, CONTRACT_FIRST,
                preferred_element_type=F32,
            ).reshape(nx, 2, half, cols)
            keep_ref[b, :, :half] = jnp.where(first, r[:, 0], r[:, 1])
            send_ref[b, :, :half] = jnp.where(first, r[:, 1], r[:, 0]).astype(BF16)
        span = pl.ds(t * per, per)
        for i, (src, dst) in enumerate(((send_ref, send_hbm), (keep_ref, keep_hbm))):
            stores.append(pltpu.make_async_copy(src.at[span], dst.at[span], out_sems.at[t, i]))
            stores[-1].start()
    for copy in stores:
        copy.wait()


def plane_sum_kernel(parts, out):
    total = parts[0].astype(F32)
    for z in range(1, parts.shape[0]):
        total = total + parts[z].astype(F32)
    out[...] = total


def squares_kernel(where_ref, flags_ref, parts, total_ref, share_ref):
    deep, cols = total_ref.shape
    wide = deep * 4 // 5
    adapters = flags_ref.shape[1]
    rank = cols // adapters
    total = jnp.sum(parts[...], axis=0)
    total_ref[...] = total
    part_a = total[:wide]
    part_b = total[wide:]
    owner = lax.broadcasted_iota(jnp.int32, part_b.shape, 0) // 4
    part_b = jnp.where(owner == where_ref[3], part_b, 0.0)
    squares = jnp.sum(part_a * part_a, axis=0, keepdims=True) + jnp.sum(
        part_b * part_b, axis=0, keepdims=True
    )
    lane = lax.broadcasted_iota(jnp.int32, (1, cols), 1)
    row = jnp.zeros((1, cols), F32)
    for e in range(adapters):
        mine = lane // rank == e
        one = jnp.sum(jnp.where(mine, squares, 0.0), axis=1, keepdims=True)
        row = jnp.where(mine, jnp.where(lane % rank == 0, one, flags_ref[0, e].astype(F32)), row)
    share_ref[...] = jnp.broadcast_to(row[None], share_ref.shape)


def adam_kernel(
    limit_sq, where_ref, total_ref, shares_ref,
    master_a, moment_a, second_a, master_b, moment_b, second_b,
    out_ma, out_oa, out_sa, out_mb, out_ob, out_sb,
):
    rows, cols = master_a.shape
    adapters = 8
    rank = cols // adapters
    row = jnp.sum(shares_ref[...], axis=0)
    lane = lax.broadcasted_iota(jnp.int32, (1, cols), 1)
    sums = jnp.zeros((1, cols), F32)
    flags = jnp.zeros((1, cols), F32)
    for e in range(adapters):
        mine = lane // rank == e
        one = jnp.sum(jnp.where(lane == e * rank, row, 0.0), axis=1, keepdims=True)
        flag = jnp.sum(jnp.where(lane == e * rank + 1, row, 0.0), axis=1, keepdims=True)
        sums = jnp.where(mine, one, sums)
        flags = jnp.where(mine, flag, flags)
    limit = jnp.sqrt(jnp.full((1, cols), limit_sq, F32))
    clip = limit / jnp.maximum(jnp.sqrt(sums), limit)
    held = flags > 0.5

    def commit(grad, master, moment, second, to_master, to_moment, to_second):
        clipped = grad * clip
        m, o, s = master[...], moment[...], second[...]
        new_o = BETA_ONE * o + (1.0 - BETA_ONE) * clipped
        new_s = BETA_TWO * s + (1.0 - BETA_TWO) * clipped * clipped
        new_m = m - LEARN_RATE * new_o / (jnp.sqrt(new_s) + ADAM_EPS)
        to_master[...] = jnp.where(held, m, new_m)
        to_moment[...] = jnp.where(held, o, new_o)
        to_second[...] = jnp.where(held, s, new_s)

    grad_a = total_ref[:rows]
    pair = total_ref[rows:]
    grad_b = jnp.where(where_ref[3] == 0, pair[:4], pair[4:])
    commit(grad_a, master_a, moment_a, second_a, out_ma, out_oa, out_sa)
    commit(grad_b, master_b, moment_b, second_b, out_mb, out_ob, out_sb)


def input_grad_kernel(
    g_hbm, weight_hbm, back_hbm, down_hbm, out_hbm, g, weight, out, sems, out_sems
):
    chunks, tile = weight.shape[:2]
    kv = g_hbm.shape[1]
    main, side = pl.ds(0, kv), pl.ds(kv, back_hbm.shape[1])
    small = [
        pltpu.make_async_copy(g_hbm, g.at[:, main], sems.at[2 * chunks]),
        pltpu.make_async_copy(back_hbm, g.at[:, side], sems.at[2 * chunks + 1]),
    ]

    def loads(i):
        rows = pl.ds(pl.multiple_of(i * tile, tile), tile)
        return (
            pltpu.make_async_copy(weight_hbm.at[rows], weight.at[i, :, main], sems.at[i]),
            pltpu.make_async_copy(down_hbm.at[rows], weight.at[i, :, side], sems.at[chunks + i]),
        )

    def store(i):
        cols = pl.ds(pl.multiple_of(i * tile, tile), tile)
        return pltpu.make_async_copy(out.at[i], out_hbm.at[:, cols], out_sems.at[i])

    for copy in small:
        copy.start()
    for i in range(chunks):
        for copy in loads(i):
            copy.start()
    for copy in small:
        copy.wait()

    def step(i, carry):
        for copy in loads(i):
            copy.wait()
        total = lax.dot_general(g[...], weight[i], CONTRACT_LAST, preferred_element_type=F32)
        out[i] = total.astype(BF16)
        store(i).start()
        return carry

    lax.fori_loop(0, chunks, step, 0)
    for i in range(chunks):
        store(i).wait()


def input_grad(g, weight, back, down, tile):
    rows, kv = g.shape
    width, cols = down.shape
    chunks = width // tile
    return pl.pallas_call(
        input_grad_kernel,
        out_shape=jax.ShapeDtypeStruct((rows, width), BF16),
        in_specs=[HBM] * 4,
        out_specs=HBM,
        scratch_shapes=[
            pltpu.VMEM((rows, kv + cols), BF16),
            pltpu.VMEM((chunks, tile, kv + cols), BF16),
            pltpu.VMEM((chunks, rows, tile), BF16),
            pltpu.SemaphoreType.DMA((2 * chunks + 2,)),
            pltpu.SemaphoreType.DMA((chunks,)),
        ],
        compiler_params=pltpu.CompilerParams(vmem_limit_bytes=60 << 20),
        cost_estimate=pl.CostEstimate(
            flops=2 * rows * width * (kv + cols),
            bytes_accessed=2 * width * (kv + cols + rows),
            transcendentals=0,
        ),
    )(g, weight, back, down)


def shift(value, axis, size, by):
    return lax.ppermute(value, axis, [(i, (i + by) % size) for i in range(size)])


def flip(value, axis, size, bit):
    return lax.ppermute(value, axis, [(i, i ^ bit) for i in range(size)])


def shards(sizes, tokens, g, base_weight, down, up, ma, oa, sa, mb, ob, sb, counts, flags):
    nz, ny, nx, nc = sizes
    rows, width = tokens.shape
    kv = g.shape[1]
    cols = down.shape[1]
    where = jnp.stack([lax.axis_index(a) for a in DEV]).astype(jnp.int32)
    sds = jax.ShapeDtypeStruct

    weight = lax.all_gather(base_weight, PLANE, axis=0, tiled=True)

    blocks = nz * ny
    deep = width // blocks // nx // nc + kv // blocks // nx
    part = (blocks, nx, deep, cols)
    tiles = 8
    keep, send, back = call(
        grads_kernel,
        (sds(part, F32), sds(part, BF16), sds((rows, cols), BF16)),
        [SMEM, SMEM, HBM, HBM, HBM, HBM],
        [
            pltpu.VMEM((rows, width), BF16),
            pltpu.VMEM((rows, kv), BF16),
            pltpu.VMEM((width, cols), BF16),
            pltpu.VMEM((kv, cols), BF16),
            pltpu.VMEM(part, F32),
            pltpu.VMEM(part, BF16),
            pltpu.SemaphoreType.DMA((tiles, 2)),
            pltpu.SemaphoreType.DMA((2,)),
            pltpu.SemaphoreType.DMA((tiles, 2)),
        ],
        limit=60,
        to=(HBM, HBM, VMEM),
        flops=4 * rows * width * cols,
        nbytes=12 << 20,
    )(where, counts, tokens, g, down, up)

    recv = flip(send, "c", nc, 1)
    to_all = (keep + recv.astype(F32)).astype(BF16)
    chips = nz * ny * nx
    from_z = lax.all_to_all(to_all.reshape(nz, ny * nx, deep, cols), "z", 0, 0, tiled=True)
    to_plane = call(plane_sum_kernel, sds((ny * nx, deep, cols), F32), [VMEM], nbytes=2 << 20)(from_z)
    from_all = lax.all_to_all(to_plane, ("y", "x"), 0, 0, tiled=True)

    total, share = call(
        squares_kernel,
        (sds((deep, cols), F32), sds((chips * nc, 1, cols), F32)),
        [SMEM, SMEM, VMEM],
    )(where, flags, from_all)
    weight, _ = lax.optimization_barrier((weight, share))
    shares = lax.all_to_all(share, DEV, 0, 0, tiled=True)
    out = input_grad(g, weight, back, down, 512)
    shares, out = lax.optimization_barrier((shares, out))

    shape = lambda v: sds(v.shape, v.dtype)
    new = call(
        functools.partial(adam_kernel, float(cols // 8 * (width + kv))),
        tuple(shape(v) for v in (ma, oa, sa, mb, ob, sb)),
        [SMEM] + [VMEM] * 8,
    )(where, total, shares, ma, oa, sa, mb, ob, sb)
    return (out, *new)


def solution(mesh):
    sizes = (8, 4, 4, 2)
    fine = Mesh(mesh.devices.reshape(sizes), DEV)
    split = P(DEV, None)
    return jax.shard_map(
        functools.partial(shards, sizes),
        mesh=fine,
        in_specs=(split, split, P(PLANE, None), P(), P()) + (split,) * 8,
        out_specs=(split,) * 7,
        check_vma=False,
    )
```

```python
import functools

import jax
import jax.numpy as jnp
from jax import lax
from jax.experimental import pallas as pl
from jax.experimental.pallas import tpu as pltpu
from jax.sharding import Mesh
from jax.sharding import PartitionSpec as P

ADAPTER_SCALE = 2.0
BETA_ONE = 0.9
BETA_TWO = 0.95
LEARN_RATE = 0.002
ADAM_EPS = 1e-08

DEV = ("far", "near", "y", "x", "c")
PLANE = ("y", "x", "c")
F32 = jnp.float32
BF16 = jnp.bfloat16
CONTRACT_LAST = (((1,), (1,)), ((), ()))
CONTRACT_FIRST = (((0,), (0,)), ((), ()))

VMEM = pl.BlockSpec(memory_space=pltpu.VMEM)
SMEM = pl.BlockSpec(memory_space=pltpu.SMEM)
HBM = pl.BlockSpec(memory_space=pl.ANY)


def call(kernel, outs, ins, scratch=(), limit=48, flops=0, nbytes=0, to=None):
    return pl.pallas_call(
        kernel,
        out_shape=outs,
        in_specs=ins,
        out_specs=jax.tree.map(lambda _: VMEM, outs) if to is None else to,
        scratch_shapes=list(scratch),
        compiler_params=pltpu.CompilerParams(vmem_limit_bytes=limit << 20),
        cost_estimate=pl.CostEstimate(flops=flops, bytes_accessed=nbytes, transcendentals=0),
    )


def grads_kernel(
    where_ref, counts_ref, tok_hbm, g_hbm, down_hbm, up_hbm,
    keep_hbm, send_hbm, back_ref,
    tok, g, down, up, keep_ref, send_ref, sems, small_sems, out_sems,
):
    rows, width = tok.shape
    kv = g.shape[1]
    cols = down.shape[1]
    adapters = counts_ref.shape[1]
    rank = cols // adapters
    tiles = sems.shape[0]
    tile = width // tiles
    blocks, nx = keep_ref.shape[:2]
    block = width // blocks
    half = block // nx // 2
    few = kv // blocks // nx
    first = where_ref[4] == 0

    g_copy = pltpu.make_async_copy(g_hbm, g, small_sems.at[0])
    up_copy = pltpu.make_async_copy(up_hbm, up, small_sems.at[1])
    g_copy.start()
    up_copy.start()
    tok_copies = []
    for t in range(tiles):
        span = pl.ds(t * tile, tile)
        a = pltpu.make_async_copy(tok_hbm.at[:, span], tok.at[:, span], sems.at[t, 0])
        b = pltpu.make_async_copy(down_hbm.at[span, :], down.at[span, :], sems.at[t, 1])
        a.start()
        b.start()
        tok_copies.append((a, b))

    row_ids = lax.broadcasted_iota(jnp.int32, (rows, cols), 0)
    col_owner = lax.broadcasted_iota(jnp.int32, (rows, cols), 1) // rank
    owner = jnp.zeros((rows, cols), jnp.int32)
    end = jnp.int32(0)
    for e in range(adapters):
        end = end + counts_ref[0, e]
        owner = owner + (row_ids >= end).astype(jnp.int32)
    mask = (owner == col_owner).astype(F32)

    g_copy.wait()
    up_copy.wait()
    back = (
        ADAPTER_SCALE * jnp.dot(g[...], up[...], preferred_element_type=F32) * mask
    ).astype(BF16)
    back_ref[...] = back

    acc = jnp.zeros((rows, cols), F32)
    for t in range(tiles):
        tok_copies[t][0].wait()
        tok_copies[t][1].wait()
        span = slice(t * tile, (t + 1) * tile)
        acc = acc + jnp.dot(tok[:, span], down[span, :], preferred_element_type=F32)
    low = (ADAPTER_SCALE * acc * mask).astype(BF16)
    group = block // (few * nx)
    for s in range(kv // block):
        r = lax.dot_general(
            g[:, s * block : (s + 1) * block], low, CONTRACT_FIRST, preferred_element_type=F32
        ).reshape(group, nx, few, cols)
        keep_ref[s * group : (s + 1) * group, :, half:] = r
        send_ref[s * group : (s + 1) * group, :, half:] = r.astype(BF16)
    per = blocks // tiles
    stores = []
    for t in range(tiles):
        for b in range(t * per, (t + 1) * per):
            r = lax.dot_general(
                tok[:, b * block : (b + 1) * block], back, CONTRACT_FIRST,
                preferred_element_type=F32,
            ).reshape(nx, 2, half, cols)
            keep_ref[b, :, :half] = jnp.where(first, r[:, 0], r[:, 1])
            send_ref[b, :, :half] = jnp.where(first, r[:, 1], r[:, 0]).astype(BF16)
        span = pl.ds(t * per, per)
        for i, (src, dst) in enumerate(((send_ref, send_hbm), (keep_ref, keep_hbm))):
            stores.append(pltpu.make_async_copy(src.at[span], dst.at[span], out_sems.at[t, i]))
            stores[-1].start()
    for copy in stores:
        copy.wait()


def split_kernel(where_ref, keep_ref, recv_ref, own_ref, up_ref, down_ref):
    near = where_ref[1]
    own_ref[0] = keep_ref[0, near] + recv_ref[0, near].astype(F32)
    other = (keep_ref[0, 1 - near] + recv_ref[0, 1 - near].astype(F32)).astype(BF16)
    low = pl.program_id(0) < pl.num_programs(0) // 2

    @pl.when(low)
    def _():
        up_ref[0] = other

    @pl.when(jnp.logical_not(low))
    def _():
        down_ref[0] = other


def split(where, keep, recv):
    count, pair = keep.shape[:2]
    rest = keep.shape[2:]
    half = count // 2
    zeros = (0,) * len(rest)
    sds = jax.ShapeDtypeStruct
    whole = pl.BlockSpec((1, pair) + rest, lambda i: (i, 0) + zeros)
    return pl.pallas_call(
        split_kernel,
        grid=(count,),
        out_shape=(
            sds((count,) + rest, F32), sds((half,) + rest, BF16), sds((half,) + rest, BF16),
        ),
        in_specs=[SMEM, whole, whole],
        out_specs=(
            pl.BlockSpec((1,) + rest, lambda i: (i,) + zeros),
            pl.BlockSpec((1,) + rest, lambda i: (jnp.minimum(i, half - 1),) + zeros),
            pl.BlockSpec((1,) + rest, lambda i: (jnp.maximum(i - half, 0),) + zeros),
        ),
        compiler_params=pltpu.CompilerParams(vmem_limit_bytes=48 << 20),
        cost_estimate=pl.CostEstimate(flops=0, bytes_accessed=6 << 20, transcendentals=0),
    )(where, keep, recv)


def merge_kernel(own_ref, low_ref, high_ref, out_ref):
    half = low_ref.shape[0]
    out_ref[:half] = (own_ref[:half] + low_ref[...].astype(F32)).astype(BF16)
    out_ref[half:] = (own_ref[half:] + high_ref[...].astype(F32)).astype(BF16)


def plane_sum_kernel(parts, out):
    total = parts[0].astype(F32)
    for z in range(1, parts.shape[0]):
        total = total + parts[z].astype(F32)
    out[...] = total


def squares_kernel(where_ref, flags_ref, parts, total_ref, share_ref):
    deep, cols = total_ref.shape
    wide = deep * 4 // 5
    adapters = flags_ref.shape[1]
    rank = cols // adapters
    total = jnp.sum(parts[...], axis=0)
    total_ref[...] = total
    part_a = total[:wide]
    part_b = total[wide:]
    owner = lax.broadcasted_iota(jnp.int32, part_b.shape, 0) // 4
    part_b = jnp.where(owner == where_ref[4], part_b, 0.0)
    squares = jnp.sum(part_a * part_a, axis=0, keepdims=True) + jnp.sum(
        part_b * part_b, axis=0, keepdims=True
    )
    lane = lax.broadcasted_iota(jnp.int32, (1, cols), 1)
    row = jnp.zeros((1, cols), F32)
    for e in range(adapters):
        mine = lane // rank == e
        one = jnp.sum(jnp.where(mine, squares, 0.0), axis=1, keepdims=True)
        row = jnp.where(mine, jnp.where(lane % rank == 0, one, flags_ref[0, e].astype(F32)), row)
    share_ref[...] = jnp.broadcast_to(row[None], share_ref.shape)


def adam_kernel(
    limit_sq, where_ref, total_ref, shares_ref,
    master_a, moment_a, second_a, master_b, moment_b, second_b,
    out_ma, out_oa, out_sa, out_mb, out_ob, out_sb,
):
    rows, cols = master_a.shape
    adapters = 8
    rank = cols // adapters
    row = jnp.sum(shares_ref[...], axis=0)
    lane = lax.broadcasted_iota(jnp.int32, (1, cols), 1)
    sums = jnp.zeros((1, cols), F32)
    flags = jnp.zeros((1, cols), F32)
    for e in range(adapters):
        mine = lane // rank == e
        one = jnp.sum(jnp.where(lane == e * rank, row, 0.0), axis=1, keepdims=True)
        flag = jnp.sum(jnp.where(lane == e * rank + 1, row, 0.0), axis=1, keepdims=True)
        sums = jnp.where(mine, one, sums)
        flags = jnp.where(mine, flag, flags)
    limit = jnp.sqrt(jnp.full((1, cols), limit_sq, F32))
    clip = limit / jnp.maximum(jnp.sqrt(sums), limit)
    held = flags > 0.5

    def commit(grad, master, moment, second, to_master, to_moment, to_second):
        clipped = grad * clip
        m, o, s = master[...], moment[...], second[...]
        new_o = BETA_ONE * o + (1.0 - BETA_ONE) * clipped
        new_s = BETA_TWO * s + (1.0 - BETA_TWO) * clipped * clipped
        new_m = m - LEARN_RATE * new_o / (jnp.sqrt(new_s) + ADAM_EPS)
        to_master[...] = jnp.where(held, m, new_m)
        to_moment[...] = jnp.where(held, o, new_o)
        to_second[...] = jnp.where(held, s, new_s)

    grad_a = total_ref[:rows]
    pair = total_ref[rows:]
    grad_b = jnp.where(where_ref[4] == 0, pair[:4], pair[4:])
    commit(grad_a, master_a, moment_a, second_a, out_ma, out_oa, out_sa)
    commit(grad_b, master_b, moment_b, second_b, out_mb, out_ob, out_sb)


def input_grad_kernel(
    g_hbm, weight_hbm, back_hbm, down_hbm, out_hbm, g, weight, out, sems, out_sems
):
    chunks, tile = weight.shape[:2]
    kv = g_hbm.shape[1]
    main, side = pl.ds(0, kv), pl.ds(kv, back_hbm.shape[1])
    small = [
        pltpu.make_async_copy(g_hbm, g.at[:, main], sems.at[2 * chunks]),
        pltpu.make_async_copy(back_hbm, g.at[:, side], sems.at[2 * chunks + 1]),
    ]

    def loads(i):
        rows = pl.ds(pl.multiple_of(i * tile, tile), tile)
        return (
            pltpu.make_async_copy(weight_hbm.at[rows], weight.at[i, :, main], sems.at[i]),
            pltpu.make_async_copy(down_hbm.at[rows], weight.at[i, :, side], sems.at[chunks + i]),
        )

    def store(i):
        cols = pl.ds(pl.multiple_of(i * tile, tile), tile)
        return pltpu.make_async_copy(out.at[i], out_hbm.at[:, cols], out_sems.at[i])

    for copy in small:
        copy.start()
    for i in range(chunks):
        for copy in loads(i):
            copy.start()
    for copy in small:
        copy.wait()

    def step(i, carry):
        for copy in loads(i):
            copy.wait()
        total = lax.dot_general(g[...], weight[i], CONTRACT_LAST, preferred_element_type=F32)
        out[i] = total.astype(BF16)
        store(i).start()
        return carry

    lax.fori_loop(0, chunks, step, 0)
    for i in range(chunks):
        store(i).wait()


def input_grad(g, weight, back, down, tile):
    rows, kv = g.shape
    width, cols = down.shape
    chunks = width // tile
    return pl.pallas_call(
        input_grad_kernel,
        out_shape=jax.ShapeDtypeStruct((rows, width), BF16),
        in_specs=[HBM] * 4,
        out_specs=HBM,
        scratch_shapes=[
            pltpu.VMEM((rows, kv + cols), BF16),
            pltpu.VMEM((chunks, tile, kv + cols), BF16),
            pltpu.VMEM((chunks, rows, tile), BF16),
            pltpu.SemaphoreType.DMA((2 * chunks + 2,)),
            pltpu.SemaphoreType.DMA((chunks,)),
        ],
        compiler_params=pltpu.CompilerParams(vmem_limit_bytes=60 << 20),
        cost_estimate=pl.CostEstimate(
            flops=2 * rows * width * (kv + cols),
            bytes_accessed=2 * width * (kv + cols + rows),
            transcendentals=0,
        ),
    )(g, weight, back, down)


def shift(value, axis, size, by):
    return lax.ppermute(value, axis, [(i, (i + by) % size) for i in range(size)])


def flip(value, axis, size, bit):
    return lax.ppermute(value, axis, [(i, i ^ bit) for i in range(size)])


def shards(sizes, tokens, g, base_weight, down, up, ma, oa, sa, mb, ob, sb, counts, flags):
    nf, nn, ny, nx, nc = sizes
    nz = nf * nn
    rows, width = tokens.shape
    kv = g.shape[1]
    cols = down.shape[1]
    where = jnp.stack([lax.axis_index(a) for a in DEV]).astype(jnp.int32)
    sds = jax.ShapeDtypeStruct

    weight = lax.all_gather(base_weight, PLANE, axis=0, tiled=True)

    blocks = nz * ny
    deep = width // blocks // nx // nc + kv // blocks // nx
    part = (blocks, nx, deep, cols)
    tiles = 8
    keep, send, back = call(
        grads_kernel,
        (sds(part, F32), sds(part, BF16), sds((rows, cols), BF16)),
        [SMEM, SMEM, HBM, HBM, HBM, HBM],
        [
            pltpu.VMEM((rows, width), BF16),
            pltpu.VMEM((rows, kv), BF16),
            pltpu.VMEM((width, cols), BF16),
            pltpu.VMEM((kv, cols), BF16),
            pltpu.VMEM(part, F32),
            pltpu.VMEM(part, BF16),
            pltpu.SemaphoreType.DMA((tiles, 2)),
            pltpu.SemaphoreType.DMA((2,)),
            pltpu.SemaphoreType.DMA((tiles, 2)),
        ],
        limit=60,
        to=(HBM, HBM, VMEM),
        flops=4 * rows * width * cols,
        nbytes=12 << 20,
    )(where, counts, tokens, g, down, up)

    recv = flip(send, "c", nc, 1)
    chips = nz * ny * nx
    fine = (nf, nn, ny * nx, deep, cols)
    own, up, low = split(where, keep.reshape(fine), recv.reshape(fine))
    z_axes = ("far", "near")
    from_below, from_above = shift(up, z_axes, nz, 1), shift(low, z_axes, nz, -1)
    merged = call(merge_kernel, sds(own.shape, BF16), [VMEM] * 3, nbytes=3 << 20)(
        own, from_below, from_above
    )
    from_far = lax.all_to_all(merged, "far", 0, 0, tiled=True)
    to_plane = call(plane_sum_kernel, sds(fine[2:], F32), [VMEM], nbytes=1 << 20)(from_far)
    from_all = lax.all_to_all(to_plane, ("y", "x"), 0, 0, tiled=True)
    total, share = call(
        squares_kernel,
        (sds((deep, cols), F32), sds((chips * nc, 1, cols), F32)),
        [SMEM, SMEM, VMEM],
    )(where, flags, from_all)
    weight, _ = lax.optimization_barrier((weight, share))
    shares = lax.all_to_all(share, DEV, 0, 0, tiled=True)
    out = input_grad(g, weight, back, down, 1024)
    shares, out = lax.optimization_barrier((shares, out))

    shape = lambda v: sds(v.shape, v.dtype)
    new = call(
        functools.partial(adam_kernel, float(cols // 8 * (width + kv))),
        tuple(shape(v) for v in (ma, oa, sa, mb, ob, sb)),
        [SMEM] + [VMEM] * 8,
    )(where, total, shares, ma, oa, sa, mb, ob, sb)
    return (out, *new)


def solution(mesh):
    sizes = (4, 2, 4, 4, 2)
    fine = Mesh(mesh.devices.reshape(sizes), DEV)
    split = P(DEV, None)
    return jax.shard_map(
        functools.partial(shards, sizes),
        mesh=fine,
        in_specs=(split, split, P(PLANE, None), P(), P()) + (split,) * 8,
        out_specs=(split,) * 7,
        check_vma=False,
    )
```

```python
import functools

import jax
import jax.numpy as jnp
from jax import lax
from jax.experimental import pallas as pl
from jax.experimental.pallas import tpu as pltpu
from jax.sharding import Mesh
from jax.sharding import PartitionSpec as P

ADAPTER_SCALE = 2.0
BETA_ONE = 0.9
BETA_TWO = 0.95
LEARN_RATE = 0.002
ADAM_EPS = 1e-08

DEV = ("far", "near", "y", "x", "c")
PLANE = ("y", "x", "c")
F32 = jnp.float32
BF16 = jnp.bfloat16
CONTRACT_LAST = (((1,), (1,)), ((), ()))
CONTRACT_FIRST = (((0,), (0,)), ((), ()))

VMEM = pl.BlockSpec(memory_space=pltpu.VMEM)
SMEM = pl.BlockSpec(memory_space=pltpu.SMEM)
HBM = pl.BlockSpec(memory_space=pl.ANY)


def call(kernel, outs, ins, scratch=(), limit=48, flops=0, nbytes=0, to=None):
    return pl.pallas_call(
        kernel,
        out_shape=outs,
        in_specs=ins,
        out_specs=jax.tree.map(lambda _: VMEM, outs) if to is None else to,
        scratch_shapes=list(scratch),
        compiler_params=pltpu.CompilerParams(vmem_limit_bytes=limit << 20),
        cost_estimate=pl.CostEstimate(flops=flops, bytes_accessed=nbytes, transcendentals=0),
    )


def grads_kernel(
    nx, where_ref, counts_ref, tok_hbm, g_hbm, down_hbm, up_hbm,
    keep_hbm, send_hbm, back_ref,
    tok, g, down, up, keep_ref, send_ref, sems, small_sems, out_sems,
):
    rows, width = tok.shape
    kv = g.shape[1]
    cols = down.shape[1]
    adapters = counts_ref.shape[1]
    rank = cols // adapters
    tiles = sems.shape[0]
    tile = width // tiles
    blocks = keep_ref.shape[0]
    block = width // blocks
    half = block // nx // 2
    few = kv // blocks // nx
    first = where_ref[4] == 0

    g_copy = pltpu.make_async_copy(g_hbm, g, small_sems.at[0])
    up_copy = pltpu.make_async_copy(up_hbm, up, small_sems.at[1])
    g_copy.start()
    up_copy.start()
    tok_copies = []
    for t in range(tiles):
        span = pl.ds(t * tile, tile)
        a = pltpu.make_async_copy(tok_hbm.at[:, span], tok.at[:, span], sems.at[t, 0])
        b = pltpu.make_async_copy(down_hbm.at[span, :], down.at[span, :], sems.at[t, 1])
        a.start()
        b.start()
        tok_copies.append((a, b))

    row_ids = lax.broadcasted_iota(jnp.int32, (rows, cols), 0)
    col_owner = lax.broadcasted_iota(jnp.int32, (rows, cols), 1) // rank
    owner = jnp.zeros((rows, cols), jnp.int32)
    end = jnp.int32(0)
    for e in range(adapters):
        end = end + counts_ref[0, e]
        owner = owner + (row_ids >= end).astype(jnp.int32)
    mask = (owner == col_owner).astype(F32)

    g_copy.wait()
    up_copy.wait()
    back = (
        ADAPTER_SCALE * jnp.dot(g[...], up[...], preferred_element_type=F32) * mask
    ).astype(BF16)
    back_ref[...] = back

    acc = jnp.zeros((rows, cols), F32)
    for t in range(tiles):
        tok_copies[t][0].wait()
        tok_copies[t][1].wait()
        span = slice(t * tile, (t + 1) * tile)
        acc = acc + jnp.dot(tok[:, span], down[span, :], preferred_element_type=F32)
    low = (ADAPTER_SCALE * acc * mask).astype(BF16)
    group = block // (few * nx)
    for s in range(kv // block):
        r = lax.dot_general(
            g[:, s * block : (s + 1) * block], low, CONTRACT_FIRST, preferred_element_type=F32
        ).reshape(group, nx * few, cols)
        keep_ref[s * group : (s + 1) * group, nx * half :] = r
        send_ref[s * group : (s + 1) * group, nx * half :] = r.astype(BF16)
    per = blocks // tiles
    stores = []
    for t in range(tiles):
        for b in range(t * per, (t + 1) * per):
            r = lax.dot_general(
                tok[:, b * block : (b + 1) * block], back, CONTRACT_FIRST,
                preferred_element_type=F32,
            ).reshape(nx, 2, half, cols)
            ours = jnp.where(first, r[:, 0], r[:, 1]).reshape(nx * half, cols)
            other = jnp.where(first, r[:, 1], r[:, 0]).reshape(nx * half, cols)
            keep_ref[b, : nx * half] = ours
            send_ref[b, : nx * half] = other.astype(BF16)
        span = pl.ds(t * per, per)
        for i, (src, dst) in enumerate(((send_ref, send_hbm), (keep_ref, keep_hbm))):
            stores.append(pltpu.make_async_copy(src.at[span], dst.at[span], out_sems.at[t, i]))
            stores[-1].start()
    for copy in stores:
        copy.wait()


def split_kernel(where_ref, keep_ref, recv_ref, own_ref, up_ref, down_ref):
    near = where_ref[1]
    own_ref[0] = keep_ref[0, near] + recv_ref[0, near].astype(F32)
    other = (keep_ref[0, 1 - near] + recv_ref[0, 1 - near].astype(F32)).astype(BF16)
    low = pl.program_id(0) < pl.num_programs(0) // 2

    @pl.when(low)
    def _():
        up_ref[0] = other

    @pl.when(jnp.logical_not(low))
    def _():
        down_ref[0] = other


def split(where, keep, recv):
    count, pair = keep.shape[:2]
    rest = keep.shape[2:]
    half = count // 2
    zeros = (0,) * len(rest)
    sds = jax.ShapeDtypeStruct
    whole = pl.BlockSpec((1, pair) + rest, lambda i: (i, 0) + zeros)
    return pl.pallas_call(
        split_kernel,
        grid=(count,),
        out_shape=(
            sds((count,) + rest, F32), sds((half,) + rest, BF16), sds((half,) + rest, BF16),
        ),
        in_specs=[SMEM, whole, whole],
        out_specs=(
            pl.BlockSpec((1,) + rest, lambda i: (i,) + zeros),
            pl.BlockSpec((1,) + rest, lambda i: (jnp.minimum(i, half - 1),) + zeros),
            pl.BlockSpec((1,) + rest, lambda i: (jnp.maximum(i - half, 0),) + zeros),
        ),
        compiler_params=pltpu.CompilerParams(vmem_limit_bytes=48 << 20),
        cost_estimate=pl.CostEstimate(flops=0, bytes_accessed=6 << 20, transcendentals=0),
    )(where, keep, recv)


def merge_kernel(where_ref, own_ref, low_ref, high_ref, out_ref, mine_ref):
    half = low_ref.shape[0]
    far = where_ref[0]
    for i in range(2 * half):
        other = low_ref[i] if i < half else high_ref[i - half]
        total = own_ref[i] + other.astype(F32)
        out_ref[i] = total.astype(BF16)

        @pl.when(far == i)
        def _():
            mine_ref[...] = total


def plane_sum_kernel(where_ref, mine_ref, parts, out):
    ny = parts.shape[1]
    chips, deep = out.shape[:2]
    nx = chips // ny
    few = deep // 5
    many = deep - few
    total = mine_ref[...]
    for z in range(parts.shape[0]):
        total = total + jnp.where(where_ref[0] == z, 0.0, parts[z].astype(F32))
    for y in range(ny):
        for x in range(nx):
            at = nx * many + x * few
            out[y * nx + x, :many] = total[y, x * many : (x + 1) * many]
            out[y * nx + x, many:] = total[y, at : at + few]


def squares_kernel(where_ref, flags_ref, parts, total_ref, share_ref):
    deep, cols = total_ref.shape
    wide = deep * 4 // 5
    adapters = flags_ref.shape[1]
    rank = cols // adapters
    total = jnp.sum(parts[...], axis=0)
    total_ref[...] = total
    part_a = total[:wide]
    part_b = total[wide:]
    owner = lax.broadcasted_iota(jnp.int32, part_b.shape, 0) // 4
    part_b = jnp.where(owner == where_ref[4], part_b, 0.0)
    squares = jnp.sum(part_a * part_a, axis=0, keepdims=True) + jnp.sum(
        part_b * part_b, axis=0, keepdims=True
    )
    lane = lax.broadcasted_iota(jnp.int32, (1, cols), 1)
    row = jnp.zeros((1, cols), F32)
    for e in range(adapters):
        mine = lane // rank == e
        one = jnp.sum(jnp.where(mine, squares, 0.0), axis=1, keepdims=True)
        row = jnp.where(mine, jnp.where(lane % rank == 0, one, flags_ref[0, e].astype(F32)), row)
    share_ref[...] = jnp.broadcast_to(row[None], share_ref.shape)


def adam_kernel(
    limit_sq, where_ref, total_ref, shares_ref,
    master_a, moment_a, second_a, master_b, moment_b, second_b,
    out_ma, out_oa, out_sa, out_mb, out_ob, out_sb,
):
    rows, cols = master_a.shape
    adapters = 8
    rank = cols // adapters
    row = jnp.sum(shares_ref[...], axis=0)
    lane = lax.broadcasted_iota(jnp.int32, (1, cols), 1)
    sums = jnp.zeros((1, cols), F32)
    flags = jnp.zeros((1, cols), F32)
    for e in range(adapters):
        mine = lane // rank == e
        one = jnp.sum(jnp.where(lane == e * rank, row, 0.0), axis=1, keepdims=True)
        flag = jnp.sum(jnp.where(lane == e * rank + 1, row, 0.0), axis=1, keepdims=True)
        sums = jnp.where(mine, one, sums)
        flags = jnp.where(mine, flag, flags)
    limit = jnp.sqrt(jnp.full((1, cols), limit_sq, F32))
    clip = limit / jnp.maximum(jnp.sqrt(sums), limit)
    held = flags > 0.5

    def commit(grad, master, moment, second, to_master, to_moment, to_second):
        clipped = grad * clip
        m, o, s = master[...], moment[...], second[...]
        new_o = BETA_ONE * o + (1.0 - BETA_ONE) * clipped
        new_s = BETA_TWO * s + (1.0 - BETA_TWO) * clipped * clipped
        new_m = m - LEARN_RATE * new_o / (jnp.sqrt(new_s) + ADAM_EPS)
        to_master[...] = jnp.where(held, m, new_m)
        to_moment[...] = jnp.where(held, o, new_o)
        to_second[...] = jnp.where(held, s, new_s)

    grad_a = total_ref[:rows]
    pair = total_ref[rows:]
    grad_b = jnp.where(where_ref[4] == 0, pair[:4], pair[4:])
    commit(grad_a, master_a, moment_a, second_a, out_ma, out_oa, out_sa)
    commit(grad_b, master_b, moment_b, second_b, out_mb, out_ob, out_sb)


def input_grad_kernel(
    g_hbm, weight_hbm, back_hbm, down_hbm, out_hbm, g, weight, out, sems, out_sems
):
    chunks, tile = weight.shape[:2]
    kv = g_hbm.shape[1]
    main, side = pl.ds(0, kv), pl.ds(kv, back_hbm.shape[1])
    small = [
        pltpu.make_async_copy(g_hbm, g.at[:, main], sems.at[2 * chunks]),
        pltpu.make_async_copy(back_hbm, g.at[:, side], sems.at[2 * chunks + 1]),
    ]

    def loads(i):
        rows = pl.ds(pl.multiple_of(i * tile, tile), tile)
        return (
            pltpu.make_async_copy(weight_hbm.at[rows], weight.at[i, :, main], sems.at[i]),
            pltpu.make_async_copy(down_hbm.at[rows], weight.at[i, :, side], sems.at[chunks + i]),
        )

    def store(i):
        cols = pl.ds(pl.multiple_of(i * tile, tile), tile)
        return pltpu.make_async_copy(out.at[i], out_hbm.at[:, cols], out_sems.at[i])

    for copy in small:
        copy.start()
    for i in range(chunks):
        for copy in loads(i):
            copy.start()
    for copy in small:
        copy.wait()

    def step(i, carry):
        for copy in loads(i):
            copy.wait()
        total = lax.dot_general(g[...], weight[i], CONTRACT_LAST, preferred_element_type=F32)
        out[i] = total.astype(BF16)
        store(i).start()
        return carry

    lax.fori_loop(0, chunks, step, 0)
    for i in range(chunks):
        store(i).wait()


def input_grad(g, weight, back, down, tile):
    rows, kv = g.shape
    width, cols = down.shape
    chunks = width // tile
    return pl.pallas_call(
        input_grad_kernel,
        out_shape=jax.ShapeDtypeStruct((rows, width), BF16),
        in_specs=[HBM] * 4,
        out_specs=HBM,
        scratch_shapes=[
            pltpu.VMEM((rows, kv + cols), BF16),
            pltpu.VMEM((chunks, tile, kv + cols), BF16),
            pltpu.VMEM((chunks, rows, tile), BF16),
            pltpu.SemaphoreType.DMA((2 * chunks + 2,)),
            pltpu.SemaphoreType.DMA((chunks,)),
        ],
        compiler_params=pltpu.CompilerParams(vmem_limit_bytes=60 << 20),
        cost_estimate=pl.CostEstimate(
            flops=2 * rows * width * (kv + cols),
            bytes_accessed=2 * width * (kv + cols + rows),
            transcendentals=0,
        ),
    )(g, weight, back, down)


def shift(value, axis, size, by):
    return lax.ppermute(value, axis, [(i, (i + by) % size) for i in range(size)])


def flip(value, axis, size, bit):
    return lax.ppermute(value, axis, [(i, i ^ bit) for i in range(size)])


def shards(sizes, tokens, g, base_weight, down, up, ma, oa, sa, mb, ob, sb, counts, flags):
    nf, nn, ny, nx, nc = sizes
    nz = nf * nn
    rows, width = tokens.shape
    kv = g.shape[1]
    cols = down.shape[1]
    where = jnp.stack([lax.axis_index(a) for a in DEV]).astype(jnp.int32)
    sds = jax.ShapeDtypeStruct

    weight = lax.all_gather(base_weight, PLANE, axis=0, tiled=True)

    blocks = nz * ny
    deep = width // blocks // nx // nc + kv // blocks // nx
    part = (blocks, nx * deep, cols)
    tiles = 8
    keep, send, back = call(
        functools.partial(grads_kernel, nx),
        (sds(part, F32), sds(part, BF16), sds((rows, cols), BF16)),
        [SMEM, SMEM, HBM, HBM, HBM, HBM],
        [
            pltpu.VMEM((rows, width), BF16),
            pltpu.VMEM((rows, kv), BF16),
            pltpu.VMEM((width, cols), BF16),
            pltpu.VMEM((kv, cols), BF16),
            pltpu.VMEM(part, F32),
            pltpu.VMEM(part, BF16),
            pltpu.SemaphoreType.DMA((tiles, 2)),
            pltpu.SemaphoreType.DMA((2,)),
            pltpu.SemaphoreType.DMA((tiles, 2)),
        ],
        limit=60,
        to=(HBM, HBM, VMEM),
        flops=4 * rows * width * cols,
        nbytes=12 << 20,
    )(where, counts, tokens, g, down, up)

    recv = flip(send, "c", nc, 1)
    chips = nz * ny * nx
    fine = (nf, nn, ny, nx * deep, cols)
    own, up, low = split(where, keep.reshape(fine), recv.reshape(fine))
    z_axes = ("far", "near")
    from_below, from_above = shift(up, z_axes, nz, 1), shift(low, z_axes, nz, -1)
    merged, mine = call(
        merge_kernel,
        (sds(own.shape, BF16), sds(own.shape[1:], F32)),
        [SMEM] + [VMEM] * 3,
        nbytes=3 << 20,
    )(where, own, from_below, from_above)
    from_far = lax.all_to_all(merged, "far", 0, 0, tiled=True)
    to_plane = call(
        plane_sum_kernel,
        sds((ny * nx, deep, cols), F32),
        [SMEM, VMEM, VMEM],
        nbytes=1 << 20,
    )(where, mine, from_far)
    from_all = lax.all_to_all(to_plane, ("y", "x"), 0, 0, tiled=True)
    total, share = call(
        squares_kernel,
        (sds((deep, cols), F32), sds((chips * nc, 1, cols), F32)),
        [SMEM, SMEM, VMEM],
    )(where, flags, from_all)
    weight, _ = lax.optimization_barrier((weight, share))
    shares = lax.all_to_all(share, DEV, 0, 0, tiled=True)
    out = input_grad(g, weight, back, down, 1024)
    shares, out = lax.optimization_barrier((shares, out))

    shape = lambda v: sds(v.shape, v.dtype)
    new = call(
        functools.partial(adam_kernel, float(cols // 8 * (width + kv))),
        tuple(shape(v) for v in (ma, oa, sa, mb, ob, sb)),
        [SMEM] + [VMEM] * 8,
    )(where, total, shares, ma, oa, sa, mb, ob, sb)
    return (out, *new)


def solution(mesh):
    sizes = (4, 2, 4, 4, 2)
    fine = Mesh(mesh.devices.reshape(sizes), DEV)
    split = P(DEV, None)
    return jax.shard_map(
        functools.partial(shards, sizes),
        mesh=fine,
        in_specs=(split, split, P(PLANE, None), P(), P()) + (split,) * 8,
        out_specs=(split,) * 7,
        check_vma=False,
    )
```

```python
import functools

import jax
import jax.numpy as jnp
from jax import lax
from jax.experimental import pallas as pl
from jax.experimental.pallas import tpu as pltpu
from jax.sharding import Mesh
from jax.sharding import PartitionSpec as P

ADAPTER_SCALE = 2.0
BETA_ONE = 0.9
BETA_TWO = 0.95
LEARN_RATE = 0.002
ADAM_EPS = 1e-08

DEV = ("far", "near", "y", "x", "c")
PLANE = ("y", "x", "c")
F32 = jnp.float32
BF16 = jnp.bfloat16
CONTRACT_LAST = (((1,), (1,)), ((), ()))
CONTRACT_FIRST = (((0,), (0,)), ((), ()))

VMEM = pl.BlockSpec(memory_space=pltpu.VMEM)
SMEM = pl.BlockSpec(memory_space=pltpu.SMEM)
HBM = pl.BlockSpec(memory_space=pl.ANY)


def call(kernel, outs, ins, scratch=(), limit=48, flops=0, nbytes=0, to=None):
    return pl.pallas_call(
        kernel,
        out_shape=outs,
        in_specs=ins,
        out_specs=jax.tree.map(lambda _: VMEM, outs) if to is None else to,
        scratch_shapes=list(scratch),
        compiler_params=pltpu.CompilerParams(vmem_limit_bytes=limit << 20),
        cost_estimate=pl.CostEstimate(flops=flops, bytes_accessed=nbytes, transcendentals=0),
    )


def grads_kernel(
    nx, where_ref, counts_ref, tok_hbm, g_hbm, down_hbm, up_hbm,
    keep_hbm, send_hbm, back_ref,
    tok, g, down, up, keep_ref, send_ref, sems, small_sems, out_sems,
):
    rows, width = tok.shape
    kv = g.shape[1]
    cols = down.shape[1]
    adapters = counts_ref.shape[1]
    rank = cols // adapters
    tiles = sems.shape[0]
    tile = width // tiles
    blocks = keep_ref.shape[0]
    block = width // blocks
    half = block // nx // 2
    few = kv // blocks // nx
    first = where_ref[4] == 0

    g_copy = pltpu.make_async_copy(g_hbm, g, small_sems.at[0])
    up_copy = pltpu.make_async_copy(up_hbm, up, small_sems.at[1])
    g_copy.start()
    up_copy.start()
    tok_copies = []
    for t in range(tiles):
        span = pl.ds(t * tile, tile)
        a = pltpu.make_async_copy(tok_hbm.at[:, span], tok.at[:, span], sems.at[t, 0])
        b = pltpu.make_async_copy(down_hbm.at[span, :], down.at[span, :], sems.at[t, 1])
        a.start()
        b.start()
        tok_copies.append((a, b))

    row_ids = lax.broadcasted_iota(jnp.int32, (rows, cols), 0)
    col_owner = lax.broadcasted_iota(jnp.int32, (rows, cols), 1) // rank
    owner = jnp.zeros((rows, cols), jnp.int32)
    end = jnp.int32(0)
    for e in range(adapters):
        end = end + counts_ref[0, e]
        owner = owner + (row_ids >= end).astype(jnp.int32)
    mask = (owner == col_owner).astype(F32)

    g_copy.wait()
    up_copy.wait()
    back = (
        ADAPTER_SCALE * jnp.dot(g[...], up[...], preferred_element_type=F32) * mask
    ).astype(BF16)
    back_ref[...] = back

    acc = jnp.zeros((rows, cols), F32)
    for t in range(tiles):
        tok_copies[t][0].wait()
        tok_copies[t][1].wait()
        span = slice(t * tile, (t + 1) * tile)
        acc = acc + jnp.dot(tok[:, span], down[span, :], preferred_element_type=F32)
    low = (ADAPTER_SCALE * acc * mask).astype(BF16)
    group = block // (few * nx)
    for s in range(kv // block):
        r = lax.dot_general(
            g[:, s * block : (s + 1) * block], low, CONTRACT_FIRST, preferred_element_type=F32
        ).reshape(group, nx * few, cols)
        keep_ref[s * group : (s + 1) * group, nx * half :] = r
        send_ref[s * group : (s + 1) * group, nx * half :] = r.astype(BF16)
    per = blocks // tiles
    stores = []
    for t in range(tiles):
        for b in range(t * per, (t + 1) * per):
            r = lax.dot_general(
                tok[:, b * block : (b + 1) * block], back, CONTRACT_FIRST,
                preferred_element_type=F32,
            ).reshape(nx, 2, half, cols)
            ours = jnp.where(first, r[:, 0], r[:, 1]).reshape(nx * half, cols)
            other = jnp.where(first, r[:, 1], r[:, 0]).reshape(nx * half, cols)
            keep_ref[b, : nx * half] = ours
            send_ref[b, : nx * half] = other.astype(BF16)
        span = pl.ds(t * per, per)
        for i, (src, dst) in enumerate(((send_ref, send_hbm), (keep_ref, keep_hbm))):
            stores.append(pltpu.make_async_copy(src.at[span], dst.at[span], out_sems.at[t, i]))
            stores[-1].start()
    for copy in stores:
        copy.wait()


def split_kernel(where_ref, keep_ref, recv_ref, own_ref, up_ref, down_ref):
    near = where_ref[1]
    own_ref[0] = keep_ref[0, near] + recv_ref[0, near].astype(F32)
    other = (keep_ref[0, 1 - near] + recv_ref[0, 1 - near].astype(F32)).astype(BF16)
    low = pl.program_id(0) < pl.num_programs(0) // 2

    @pl.when(low)
    def _():
        up_ref[0] = other

    @pl.when(jnp.logical_not(low))
    def _():
        down_ref[0] = other


def split(where, keep, recv):
    count, pair = keep.shape[:2]
    rest = keep.shape[2:]
    half = count // 2
    zeros = (0,) * len(rest)
    sds = jax.ShapeDtypeStruct
    whole = pl.BlockSpec((1, pair) + rest, lambda i: (i, 0) + zeros)
    return pl.pallas_call(
        split_kernel,
        grid=(count,),
        out_shape=(
            sds((count,) + rest, F32), sds((half,) + rest, BF16), sds((half,) + rest, BF16),
        ),
        in_specs=[SMEM, whole, whole],
        out_specs=(
            pl.BlockSpec((1,) + rest, lambda i: (i,) + zeros),
            pl.BlockSpec((1,) + rest, lambda i: (jnp.minimum(i, half - 1),) + zeros),
            pl.BlockSpec((1,) + rest, lambda i: (jnp.maximum(i - half, 0),) + zeros),
        ),
        compiler_params=pltpu.CompilerParams(vmem_limit_bytes=48 << 20),
        cost_estimate=pl.CostEstimate(flops=0, bytes_accessed=6 << 20, transcendentals=0),
    )(where, keep, recv)


def merge_kernel(where_ref, own_ref, low_ref, high_ref, out_ref, mine_ref):
    half = low_ref.shape[0]
    far = where_ref[0]
    for i in range(2 * half):
        other = low_ref[i] if i < half else high_ref[i - half]
        total = own_ref[i] + other.astype(F32)
        out_ref[i] = total.astype(BF16)

        @pl.when(far == i)
        def _():
            mine_ref[...] = total


def plane_sum_kernel(where_ref, mine_ref, parts, out):
    ny = parts.shape[1]
    chips, deep = out.shape[:2]
    nx = chips // ny
    few = deep // 5
    many = deep - few
    total = mine_ref[...]
    for z in range(parts.shape[0]):
        total = total + jnp.where(where_ref[0] == z, 0.0, parts[z].astype(F32))
    for y in range(ny):
        for x in range(nx):
            at = nx * many + x * few
            out[y * nx + x, :many] = total[y, x * many : (x + 1) * many]
            out[y * nx + x, many:] = total[y, at : at + few]


def squares_kernel(where_ref, flags_ref, parts, total_ref, share_ref):
    deep, cols = total_ref.shape
    wide = deep * 4 // 5
    adapters = flags_ref.shape[1]
    rank = cols // adapters
    total = jnp.sum(parts[...], axis=0)
    total_ref[...] = total
    part_a = total[:wide]
    part_b = total[wide:]
    owner = lax.broadcasted_iota(jnp.int32, part_b.shape, 0) // 4
    part_b = jnp.where(owner == where_ref[4], part_b, 0.0)
    squares = jnp.sum(part_a * part_a, axis=0, keepdims=True) + jnp.sum(
        part_b * part_b, axis=0, keepdims=True
    )
    lane = lax.broadcasted_iota(jnp.int32, (1, cols), 1)
    row = jnp.zeros((1, cols), F32)
    for e in range(adapters):
        mine = lane // rank == e
        one = jnp.sum(jnp.where(mine, squares, 0.0), axis=1, keepdims=True)
        row = jnp.where(mine, jnp.where(lane % rank == 0, one, flags_ref[0, e].astype(F32)), row)
    share_ref[...] = jnp.broadcast_to(row[None], share_ref.shape)


def adam_kernel(
    limit_sq, where_ref, total_ref, shares_ref,
    master_a, moment_a, second_a, master_b, moment_b, second_b,
    out_ma, out_oa, out_sa, out_mb, out_ob, out_sb,
):
    rows, cols = master_a.shape
    adapters = 8
    rank = cols // adapters
    row = jnp.sum(shares_ref[...], axis=0)
    lane = lax.broadcasted_iota(jnp.int32, (1, cols), 1)
    sums = jnp.zeros((1, cols), F32)
    flags = jnp.zeros((1, cols), F32)
    for e in range(adapters):
        mine = lane // rank == e
        one = jnp.sum(jnp.where(lane == e * rank, row, 0.0), axis=1, keepdims=True)
        flag = jnp.sum(jnp.where(lane == e * rank + 1, row, 0.0), axis=1, keepdims=True)
        sums = jnp.where(mine, one, sums)
        flags = jnp.where(mine, flag, flags)
    limit = jnp.sqrt(jnp.full((1, cols), limit_sq, F32))
    clip = limit / jnp.maximum(jnp.sqrt(sums), limit)
    held = flags > 0.5

    def commit(grad, master, moment, second, to_master, to_moment, to_second):
        clipped = grad * clip
        m, o, s = master[...], moment[...], second[...]
        new_o = BETA_ONE * o + (1.0 - BETA_ONE) * clipped
        new_s = BETA_TWO * s + (1.0 - BETA_TWO) * clipped * clipped
        new_m = m - LEARN_RATE * new_o / (jnp.sqrt(new_s) + ADAM_EPS)
        to_master[...] = jnp.where(held, m, new_m)
        to_moment[...] = jnp.where(held, o, new_o)
        to_second[...] = jnp.where(held, s, new_s)

    grad_a = total_ref[:rows]
    pair = total_ref[rows:]
    grad_b = jnp.where(where_ref[4] == 0, pair[:4], pair[4:])
    commit(grad_a, master_a, moment_a, second_a, out_ma, out_oa, out_sa)
    commit(grad_b, master_b, moment_b, second_b, out_mb, out_ob, out_sb)


def input_grad_kernel(
    g_hbm, weight_hbm, back_hbm, down_hbm, out_hbm, g, weight, out, sems, out_sems
):
    chunks, tile = weight.shape[:2]
    kv = g_hbm.shape[1]
    main, side = pl.ds(0, kv), pl.ds(kv, back_hbm.shape[1])
    small = [
        pltpu.make_async_copy(g_hbm, g.at[:, main], sems.at[2 * chunks]),
        pltpu.make_async_copy(back_hbm, g.at[:, side], sems.at[2 * chunks + 1]),
    ]

    def loads(i):
        rows = pl.ds(pl.multiple_of(i * tile, tile), tile)
        return (
            pltpu.make_async_copy(weight_hbm.at[rows], weight.at[i, :, main], sems.at[i]),
            pltpu.make_async_copy(down_hbm.at[rows], weight.at[i, :, side], sems.at[chunks + i]),
        )

    def store(i):
        cols = pl.ds(pl.multiple_of(i * tile, tile), tile)
        return pltpu.make_async_copy(out.at[i], out_hbm.at[:, cols], out_sems.at[i])

    for copy in small:
        copy.start()
    for i in range(chunks):
        for copy in loads(i):
            copy.start()
    for copy in small:
        copy.wait()

    def step(i, carry):
        for copy in loads(i):
            copy.wait()
        total = lax.dot_general(g[...], weight[i], CONTRACT_LAST, preferred_element_type=F32)
        out[i] = total.astype(BF16)
        store(i).start()
        return carry

    lax.fori_loop(0, chunks, step, 0)
    for i in range(chunks):
        store(i).wait()


def input_grad(g, weight, back, down, tile):
    rows, kv = g.shape
    width, cols = down.shape
    chunks = width // tile
    return pl.pallas_call(
        input_grad_kernel,
        out_shape=jax.ShapeDtypeStruct((rows, width), BF16),
        in_specs=[HBM] * 4,
        out_specs=HBM,
        scratch_shapes=[
            pltpu.VMEM((rows, kv + cols), BF16),
            pltpu.VMEM((chunks, tile, kv + cols), BF16),
            pltpu.VMEM((chunks, rows, tile), BF16),
            pltpu.SemaphoreType.DMA((2 * chunks + 2,)),
            pltpu.SemaphoreType.DMA((chunks,)),
        ],
        compiler_params=pltpu.CompilerParams(vmem_limit_bytes=52 << 20),
        cost_estimate=pl.CostEstimate(
            flops=2 * rows * width * (kv + cols),
            bytes_accessed=2 * width * (kv + cols + rows),
            transcendentals=0,
        ),
    )(g, weight, back, down)


def shift(value, axis, size, by):
    return lax.ppermute(value, axis, [(i, (i + by) % size) for i in range(size)])


def flip(value, axis, size, bit):
    return lax.ppermute(value, axis, [(i, i ^ bit) for i in range(size)])


def shards(sizes, tokens, g, base_weight, down, up, ma, oa, sa, mb, ob, sb, counts, flags):
    nf, nn, ny, nx, nc = sizes
    nz = nf * nn
    rows, width = tokens.shape
    kv = g.shape[1]
    cols = down.shape[1]
    where = jnp.stack([lax.axis_index(a) for a in DEV]).astype(jnp.int32)
    sds = jax.ShapeDtypeStruct

    weight = lax.all_gather(base_weight, PLANE, axis=0, tiled=True)

    blocks = nz * ny
    deep = width // blocks // nx // nc + kv // blocks // nx
    part = (blocks, nx * deep, cols)
    tiles = 8
    keep, send, back = call(
        functools.partial(grads_kernel, nx),
        (sds(part, F32), sds(part, BF16), sds((rows, cols), BF16)),
        [SMEM, SMEM, HBM, HBM, HBM, HBM],
        [
            pltpu.VMEM((rows, width), BF16),
            pltpu.VMEM((rows, kv), BF16),
            pltpu.VMEM((width, cols), BF16),
            pltpu.VMEM((kv, cols), BF16),
            pltpu.VMEM(part, F32),
            pltpu.VMEM(part, BF16),
            pltpu.SemaphoreType.DMA((tiles, 2)),
            pltpu.SemaphoreType.DMA((2,)),
            pltpu.SemaphoreType.DMA((tiles, 2)),
        ],
        limit=60,
        to=(HBM, HBM, VMEM),
        flops=4 * rows * width * cols,
        nbytes=12 << 20,
    )(where, counts, tokens, g, down, up)

    recv = flip(send, "c", nc, 1)
    chips = nz * ny * nx
    fine = (nf, nn, ny, nx * deep, cols)
    own, up, low = split(where, keep.reshape(fine), recv.reshape(fine))
    z_axes = ("far", "near")
    from_below, from_above = shift(up, z_axes, nz, 1), shift(low, z_axes, nz, -1)
    merged, mine = call(
        merge_kernel,
        (sds(own.shape, BF16), sds(own.shape[1:], F32)),
        [SMEM] + [VMEM] * 3,
        nbytes=3 << 20,
    )(where, own, from_below, from_above)
    from_far = lax.all_to_all(merged, "far", 0, 0, tiled=True)
    to_plane = call(
        plane_sum_kernel,
        sds((ny * nx, deep, cols), F32),
        [SMEM, VMEM, VMEM],
        nbytes=1 << 20,
    )(where, mine, from_far)
    from_all = lax.all_to_all(to_plane, ("y", "x"), 0, 0, tiled=True)
    total, share = call(
        squares_kernel,
        (sds((deep, cols), F32), sds((chips * nc, 1, cols), F32)),
        [SMEM, SMEM, VMEM],
    )(where, flags, from_all)
    weight, _ = lax.optimization_barrier((weight, share))
    shares = lax.all_to_all(share, DEV, 0, 0, tiled=True)
    out = input_grad(g, weight, back, down, 1024)
    shares, out = lax.optimization_barrier((shares, out))

    shape = lambda v: sds(v.shape, v.dtype)
    new = call(
        functools.partial(adam_kernel, float(cols // 8 * (width + kv))),
        tuple(shape(v) for v in (ma, oa, sa, mb, ob, sb)),
        [SMEM] + [VMEM] * 8,
    )(where, total, shares, ma, oa, sa, mb, ob, sb)
    return (out, *new)


def solution(mesh):
    sizes = (4, 2, 4, 4, 2)
    fine = Mesh(mesh.devices.reshape(sizes), DEV)
    split = P(DEV, None)
    return jax.shard_map(
        functools.partial(shards, sizes),
        mesh=fine,
        in_specs=(split, split, P(PLANE, None), P(), P()) + (split,) * 8,
        out_specs=(split,) * 7,
        check_vma=False,
    )
```
